128 devices in a mesh: box: 16 (over x, y), dir: 8 (over z, core).
Axes of the slice: x: 4, y: 4, z: 4, core: 2. Of those that a mesh axis runs over, the one named last changes fastest.
Arguments:
- currents: bfloat16 [2, 32, 8, 16384], P(None, None, None, ('box', 'dir')), may hold values from -6 to 6
- neighbour_impedance_tiles: bfloat16 [2, 16, 32, 32, 16384], P(None, None, None, None, ('box', 'dir')), may hold values from -0.25 to 0.25
- near_index: int32 [16, 16384], P(None, ('box', 'dir')), may hold values from 0 to 16383, as said below
- near_count: int32 [16384], P(('box', 'dir')), may hold values from 1 to 16
- radiation: bfloat16 [2, 128, 32], replicated, may hold values from -0.75 to 0.75
- interp: bfloat16 [512, 128], replicated, may hold values from -0.25 to 0.25
- shift_phase: float32 [2, 8, 128], replicated, may hold values from -1 to 1, as said below
- trans_table: float32 [2, 316, 512], replicated, may hold values from -1.5 to 1.5
- trans_kind: int32 [16, 2048], replicated, may hold values from 0 to 315
- trans_target: int32 [16, 2048], replicated, may hold values from 0 to 2047, as said below
- inter_count: int32 [2048], replicated, may hold values from 1 to 16
Outputs:
- field: float32 [2, 32, 8, 16384], P(None, None, None, ('box', 'dir'))
The draws below stay inside these ranges and needn't reach their ends.
Inputs may be any that keep to these rules, and one draw needn't show every extreme that they name: near_index[p, b] differs from b by at most 128, and by exactly 128 for some slots; near_index[0, b] = b. trans_target[s, P] is never P. Each pair shift_phase[0, o, q], shift_phase[1, o, q] has modulus one.
All inputs are finite; a program needn't handle non-finite values.
Results may differ from the reference program's by a relative error of at most 0.0054.
Values may be sent and summed in bfloat16 or wider, within the bound.
No kernel may reach another device: no remote copies, remote signals or barrier semaphores. Data moves between devices by JAX's collectives and lax.ppermute only.
A program may use at most 192 MiB of HBM per device.

```python
import math
import jax
import jax.numpy as jnp
from jax import lax

BASIS = 32
RHS = 8
Q_A = 128
Q_B = 512
NEAR = 16
ILIST = 16
KINDS = 316
BOX_DEV = 128
BOXES = 16384
PARENTS = 2048
PB_BOX = 128


def draw_near_index(key, part):
    key = jax.random.fold_in(key, 11)
    box_ids = jnp.arange(BOXES, dtype=jnp.int32)
    offsets = jax.random.randint(key, (NEAR, BOXES), -BOX_DEV, BOX_DEV + 1, dtype=jnp.int32)
    furthest = jnp.where(box_ids + BOX_DEV < BOXES, BOX_DEV, -BOX_DEV).astype(jnp.int32)
    offsets = offsets.at[NEAR - 1].set(jnp.where(box_ids % 7 == 3, furthest, offsets[NEAR - 1]))
    offsets = offsets.at[0].set(jnp.zeros((BOXES,), jnp.int32))
    return jnp.clip(box_ids[None, :] + offsets, 0, BOXES - 1).astype(jnp.int32)


def draw_near_count(key, part):
    key = jax.random.fold_in(key, 12)
    device_key, value_key = jax.random.split(key)
    box_ids = jnp.arange(BOXES, dtype=jnp.int32)
    heavy = jax.random.randint(device_key, (BOXES // BOX_DEV,), 0, 4, dtype=jnp.int32) == 0
    flagged = heavy[box_ids // BOX_DEV]
    low_end = jnp.where(flagged, NEAR // 2, 1).astype(jnp.int32)
    high_end = jnp.where(flagged, NEAR + 1, NEAR // 2 + 1).astype(jnp.int32)
    counts = jax.random.randint(value_key, (BOXES,), low_end, high_end, dtype=jnp.int32)
    return jnp.where(box_ids % 5 == 0, NEAR, counts).astype(jnp.int32)


def draw_trans_target(key, part):
    key = jax.random.fold_in(key, 13)
    parent_ids = jnp.arange(PARENTS, dtype=jnp.int32)
    offsets = jax.random.randint(key, (ILIST, PARENTS), 1, PARENTS, dtype=jnp.int32)
    offsets = offsets.at[0].set(jnp.where(parent_ids < 2, PARENTS - 1, offsets[0]).astype(jnp.int32))
    return ((parent_ids[None, :] + offsets) % PARENTS).astype(jnp.int32)


def draw_inter_count(key, part):
    key = jax.random.fold_in(key, 14)
    parent_ids = jnp.arange(PARENTS, dtype=jnp.int32)
    counts = jax.random.randint(key, (PARENTS,), 1, ILIST + 1, dtype=jnp.int32)
    return jnp.where(parent_ids % 5 == 0, ILIST, counts).astype(jnp.int32)


def draw_shift_phase(key, part):
    key = jax.random.fold_in(key, 15)
    angles = jax.random.uniform(key, (8, Q_A), jnp.float32, -math.pi, math.pi)
    return jnp.stack([jnp.cos(angles), jnp.sin(angles)]).astype(jnp.float32)


def place_ends(drawn, stream_key, least, largest):
    longest = drawn.shape.index(max(drawn.shape))
    spots = []
    for shift in (0, 1):
        where = [jax.random.randint(jax.random.fold_in(stream_key, axis), (), 0, length) for axis, length in enumerate(drawn.shape)]
        where[longest] = (where[longest] + shift) % drawn.shape[longest]
        spots.append(tuple(where))
    return drawn.at[spots[0]].set(least).at[spots[1]].set(largest)


def shard_levels(own_key, extent, pieces, low, top_value):
    gain, own = 1.0, jax.random.fold_in(own_key, 6)
    for position, shards_of in pieces:
        steps = jnp.exp(jax.random.uniform(jax.random.fold_in(own, position), (shards_of,), jnp.float32, low / len(pieces), top_value / len(pieces)))
        gain = gain * jnp.repeat(steps, extent[position] // shards_of).reshape([-1 if axis == position else 1 for axis in range(len(extent))])
    return gain


def bell_draw(own_key, dims, scale, reach, shards=(), kind=jnp.bfloat16):
    drawn = scale * jax.random.normal(own_key, dims, jnp.float32)
    if shards:
        drawn = drawn * shard_levels(own_key, dims, shards, -0.22, 0.18)
    return jnp.clip(drawn, -reach, reach).astype(kind)


def setup_inputs(seed: int = 0) -> dict:
    keys = jax.random.split(jax.random.key(seed), 12)
    currents = bell_draw(keys[0], (2, BASIS, RHS, BOXES), 1.0, 6.0, ((3, 128),))
    neighbour_impedance_tiles = bell_draw(keys[1], (2, NEAR, BASIS, BASIS, BOXES), (NEAR * BASIS) ** -0.5, 0.25, ((4, 128),))
    near_index = draw_near_index(jax.random.fold_in(keys[11], 71), 0)
    near_count = draw_near_count(jax.random.fold_in(keys[11], 71), 0)
    radiation = bell_draw(keys[4], (2, Q_A, BASIS), (2 * BASIS) ** -0.5, 0.75)
    interp = bell_draw(keys[5], (Q_B, Q_A), Q_B ** -0.5, 0.25)
    shift_phase = draw_shift_phase(jax.random.fold_in(keys[11], 71), 0)
    trans_table = bell_draw(keys[7], (2, KINDS, Q_B), ILIST ** -0.5, 1.5, (), jnp.float32)
    trans_kind = place_ends(jax.random.randint(keys[8], (ILIST, PARENTS), 0, KINDS), jax.random.fold_in(keys[8], 1), 0, KINDS - 1).astype(jnp.int32)
    trans_target = draw_trans_target(jax.random.fold_in(keys[11], 71), 0)
    inter_count = draw_inter_count(jax.random.fold_in(keys[11], 71), 0)
    return {"currents": currents, "neighbour_impedance_tiles": neighbour_impedance_tiles, "near_index": near_index, "near_count": near_count, "radiation": radiation, "interp": interp, "shift_phase": shift_phase, "trans_table": trans_table, "trans_kind": trans_kind, "trans_target": trans_target, "inter_count": inter_count}


def phasor_product(form, operator_matrix, vector):
    mat_re = operator_matrix[0].astype(jnp.float32)
    mat_im = operator_matrix[1].astype(jnp.float32)
    vec_re = vector[0].astype(jnp.float32)
    vec_im = vector[1].astype(jnp.float32)
    real_part = jnp.einsum(form, mat_re, vec_re) - jnp.einsum(form, mat_im, vec_im)
    imag_part = jnp.einsum(form, mat_re, vec_im) + jnp.einsum(form, mat_im, vec_re)
    return jnp.stack([real_part, imag_part])


def octant_sum(leaf, shift_phase):
    groups = leaf.reshape(leaf.shape[0], leaf.shape[1], leaf.shape[2], leaf.shape[3] // 8, 8)
    phase_re = jnp.transpose(shift_phase[0])[:, None, None, :]
    phase_im = jnp.transpose(shift_phase[1])[:, None, None, :]
    real_part = jnp.sum(phase_re * groups[0] - phase_im * groups[1], axis=-1)
    imag_part = jnp.sum(phase_re * groups[1] + phase_im * groups[0], axis=-1)
    return jnp.stack([real_part, imag_part]).astype(jnp.bfloat16)


def spread_children(anter, shift_phase):
    phase_re = jnp.transpose(shift_phase[0])[:, None, None, :]
    phase_im = jnp.transpose(shift_phase[1])[:, None, None, :]
    anter_re = anter[0][..., None]
    anterpolation_imaginary = anter[1][..., None]
    real_part = phase_re * anter_re + phase_im * anterpolation_imaginary
    imag_part = phase_re * anterpolation_imaginary - phase_im * anter_re
    shape = (anter.shape[1], anter.shape[2], anter.shape[3] * 8)
    return jnp.stack([real_part.reshape(shape), imag_part.reshape(shape)]).astype(jnp.bfloat16)


def translate(partial_total, fraction_piece, first, table_part, kinds, targets, counts, lowest):
    count_rows = fraction_piece.shape[3]
    width = partial_total.shape[3]
    kind_rows = lax.dynamic_slice_in_dim(kinds, first, count_rows, 1)
    target_rows = lax.dynamic_slice_in_dim(targets, first, count_rows, 1) - lowest
    used_rows = lax.dynamic_slice_in_dim(counts, first, count_rows, 0)
    source = fraction_piece.astype(jnp.float32)

    def slot_step(slot, total):
        kind_one = lax.dynamic_index_in_dim(kind_rows, slot, 0, False)
        target_one = lax.dynamic_index_in_dim(target_rows, slot, 0, False)
        inside = (slot < used_rows) & (target_one >= 0) & (target_one < width)
        weight = inside.astype(jnp.float32)
        picked = jnp.moveaxis(jnp.take(table_part, kind_one, axis=1), 1, 2)
        factor = picked * weight[None, None, :]
        factor_re = factor[0][:, None, :]
        factor_im = factor[1][:, None, :]
        real_part = factor_re * source[0] - factor_im * source[1]
        imag_part = factor_re * source[1] + factor_im * source[0]
        placed = jnp.clip(target_one, 0, width - 1)
        return total.at[:, :, :, placed].add(jnp.stack([real_part, imag_part]))

    return lax.fori_loop(0, kinds.shape[0], slot_step, partial_total)


def reference(currents, neighbour_impedance_tiles, near_index, near_count, radiation, interp, shift_phase, trans_table, trans_kind, trans_target, inter_count):
    block_count = BOXES // BOX_DEV

    def near_block(number):
        first = number * BOX_DEV
        panel_pile_entries = lax.dynamic_slice_in_dim(neighbour_impedance_tiles, first, BOX_DEV, 4)
        indices = lax.dynamic_slice_in_dim(near_index, first, BOX_DEV, 1)
        used = lax.dynamic_slice_in_dim(near_count, first, BOX_DEV, 0)
        gathered_entries = jnp.take(currents, indices, axis=3).astype(jnp.float32)
        slots = jnp.arange(NEAR, dtype=jnp.int32)[:, None]
        gathered_entries = gathered_entries * (slots < used[None, :]).astype(jnp.float32)
        return phasor_product("xoyu,ohxu->yhu", panel_pile_entries, gathered_entries)

    neighbour_pieces = lax.map(near_block, jnp.arange(block_count, dtype=jnp.int32))
    neighbour_contribution = jnp.moveaxis(neighbour_pieces, 0, 3).reshape(2, BASIS, RHS, BOXES)

    leaf = phasor_product("qn,nrb->qrb", radiation, currents)
    shifted = octant_sum(leaf, shift_phase)
    parent = jnp.einsum("kq,cqrb->ckrb", interp.astype(jnp.float32), shifted.astype(jnp.float32)).astype(jnp.bfloat16)

    partial_total = jnp.zeros((2, Q_B, RHS, PARENTS), jnp.float32)

    def block_step(number, partial_total):
        first = jnp.asarray(number, jnp.int32) * PB_BOX
        fraction_piece = lax.dynamic_slice_in_dim(parent, first, PB_BOX, 3)
        return translate(partial_total, fraction_piece, first, trans_table, trans_kind, trans_target, inter_count, 0)

    partial_total = lax.fori_loop(0, PARENTS // PB_BOX, block_step, partial_total)
    incoming = partial_total.astype(jnp.bfloat16)
    anter = jnp.einsum("kq,ckrb->cqrb", interp.astype(jnp.float32), incoming.astype(jnp.float32))
    received = spread_children(anter, shift_phase)
    far_term = phasor_product("qn,qrb->nrb", radiation, received)
    return neighbour_contribution + far_term
```

```python
import functools

import jax
import jax.numpy as jnp
from jax import lax
from jax.experimental import pallas as pl
from jax.experimental.pallas import tpu as pltpu
from jax.sharding import PartitionSpec as P

F32 = jnp.float32
BF16 = jnp.bfloat16
ALL = ("box", "dir")
VMEM_LIMIT = 48 * 1024 * 1024


def vmem_spec():
    return pl.BlockSpec(memory_space=pltpu.VMEM)


def params(**more):
    return pltpu.CompilerParams(vmem_limit_bytes=VMEM_LIMIT, **more)


def dot(a, b, dims):
    return lax.dot_general(a, b, (dims, ((), ())), preferred_element_type=F32)


def leaf_kernel(cur_ref, rad_ref, phase_ref, out_ref, wide_ref):
    rhs, parents, _ = out_ref.shape
    rows = cur_ref.shape[0] // rhs
    wide_ref[...] = cur_ref[...].astype(F32)
    rad_re, rad_im = rad_ref[0], rad_ref[1]
    operator = jnp.concatenate(
        [
            jnp.concatenate([rad_re, rad_im], axis=1),
            jnp.concatenate([-rad_im, rad_re], axis=1),
        ],
        axis=0,
    )
    samples = rad_re.shape[1]
    phase_re, phase_im = phase_ref[0][None], phase_ref[1][None]
    for r in range(rhs):
        vector = wide_ref[pl.ds(r, rows, stride=rhs), :].astype(BF16)
        leaf = dot(vector, operator, ((0,), (0,)))
        leaf_re = leaf[:, :samples].reshape(parents, 8, samples)
        leaf_im = leaf[:, samples:].reshape(parents, 8, samples)
        shifted_re = jnp.sum(phase_re * leaf_re - phase_im * leaf_im, axis=1)
        shifted_im = jnp.sum(phase_re * leaf_im + phase_im * leaf_re, axis=1)
        out_ref[r] = jnp.concatenate([shifted_re, shifted_im], axis=1).astype(BF16)


def translate_kernel(box_ref, src_ref, interp_ref, table_ref, kind_ref, target_ref, count_ref, out_ref, pair_ref, hot_ref):
    sources, double = src_ref.shape
    samples = double // 2
    slots = kind_ref.shape[0]
    targets = out_ref.shape[0]
    fine = interp_ref.shape[0]
    kinds = table_ref.shape[0]
    interp = interp_ref[...]
    parent_re = dot(src_ref[:, :samples], interp, ((1,), (1,))).astype(BF16).astype(F32)
    parent_im = dot(src_ref[:, samples:], interp, ((1,), (1,))).astype(BF16).astype(F32)
    kind_columns = jnp.transpose(kind_ref[...].astype(F32)).astype(jnp.int32)
    kind_iota = lax.broadcasted_iota(jnp.int32, (sources, kinds), 1)
    target_iota = lax.broadcasted_iota(jnp.int32, (targets, sources), 0)
    count = count_ref[...]
    for s in range(slots):
        hot = (kind_iota == kind_columns[:, s : s + 1]).astype(F32).astype(BF16)
        factor = dot(hot, table_ref[...], ((1,), (0,)))
        factor_re, factor_im = factor[:, :fine], factor[:, fine:]
        real_part = (factor_re * parent_re - factor_im * parent_im).astype(BF16)
        imag_part = (factor_re * parent_im + factor_im * parent_re).astype(BF16)
        rows = pl.ds(s * sources, sources)
        pair_ref[rows, :samples] = dot(real_part, interp, ((1,), (0,))).astype(BF16)
        pair_ref[rows, samples:] = dot(imag_part, interp, ((1,), (0,))).astype(BF16)
        target = jnp.where(s < count, target_ref[s : s + 1, :], -1)
        hot_ref[:, rows] = (target_iota == target).astype(F32).astype(BF16)
    step = 512
    for t in range(0, targets, step):
        total = dot(hot_ref[pl.ds(t, step), :], pair_ref[...], ((1,), (0,)))
        out_ref[pl.ds(t, step), :] = total.astype(BF16)


def near_kernel(first, base_ref, before_ref, cur_ref, after_ref, index_ref, count_ref, tiles_ref, *rest):
    if first:
        out_ref, all_ref, field_ref, sum_ref = rest
    else:
        given_ref, out_ref, all_ref, field_ref, sum_ref = rest
    slot = pl.program_id(0)
    boxes = cur_ref.shape[1]
    basis = tiles_ref.shape[2]
    rhs = cur_ref.shape[0] // (2 * basis)

    @pl.when(slot == 0)
    def _():
        all_ref[:, :boxes] = before_ref[...]
        all_ref[:, boxes : 2 * boxes] = cur_ref[...]
        all_ref[:, 2 * boxes :] = after_ref[...]
        sum_ref[...] = jnp.zeros_like(sum_ref)

    number = first_slot(first) + slot
    index = index_ref[pl.ds(number, 1), :] - (base_ref[0] - boxes)
    index = jnp.where(number < count_ref[...], index, -1)
    iota = lax.broadcasted_iota(jnp.int32, (3 * boxes, boxes), 0)
    hot = (iota == index).astype(F32).astype(BF16)
    picked = dot(all_ref[...], hot, ((1,), (0,)))
    half = basis * rhs
    vec_re, vec_im = picked[:half], picked[half:]
    field_ref[0] = vec_re
    field_ref[1] = vec_im - vec_re
    field_ref[2] = vec_re + vec_im

    for mb in range(0, basis, 16):
        for rb in range(0, rhs, 4):

            def step(n, sums):
                tile_re = tiles_ref[0, 0, n, pl.ds(mb, 16), :].astype(F32)
                tile_im = tiles_ref[1, 0, n, pl.ds(mb, 16), :].astype(F32)
                tile_sum = tile_re + tile_im
                sums = list(sums)
                for j in range(4):
                    row = pl.ds(n * rhs + rb + j, 1)
                    sums[3 * j] += tile_sum * field_ref[0, row, :]
                    sums[3 * j + 1] += tile_re * field_ref[1, row, :]
                    sums[3 * j + 2] += tile_im * field_ref[2, row, :]
                return tuple(sums)

            zero = jnp.zeros((16, boxes), F32)
            sums = lax.fori_loop(0, basis, step, (zero,) * 12, unroll=4)
            for j in range(4):
                sum_ref[0, rb + j, pl.ds(mb, 16), :] += sums[3 * j] - sums[3 * j + 2]
                sum_ref[1, rb + j, pl.ds(mb, 16), :] += sums[3 * j] + sums[3 * j + 1]

    @pl.when(slot == pl.num_programs(0) - 1)
    def _():
        for c in range(2):
            for r in range(rhs):
                rows = pl.ds(c * half + r, basis, stride=rhs)
                if first:
                    out_ref[rows, :] = sum_ref[c, r]
                else:
                    out_ref[rows, :] = sum_ref[c, r] + given_ref[rows, :]


FIRST_SLOTS = 4


def first_slot(first):
    return 0 if first else FIRST_SLOTS


def field_kernel(part_ref, rad_ref, phase_ref, near_ref, out_ref):
    devices, parents, double = part_ref.shape
    samples = double // 2
    rhs = 8
    rad_re, rad_im = rad_ref[0], rad_ref[1]
    operator = jnp.concatenate(
        [
            jnp.concatenate([rad_re, -rad_im], axis=1),
            jnp.concatenate([rad_im, rad_re], axis=1),
        ],
        axis=0,
    )
    rows = operator.shape[0]
    phase_re, phase_im = phase_ref[0][None], phase_ref[1][None]
    for r in range(rhs):
        anter = part_ref[r].astype(F32)
        for i in range(r + rhs, devices, rhs):
            anter += part_ref[i].astype(F32)
        anter_re = anter[:, None, :samples]
        anter_im = anter[:, None, samples:]
        real_part = phase_re * anter_re + phase_im * anter_im
        imag_part = phase_re * anter_im - phase_im * anter_re
        received = jnp.concatenate(
            [
                real_part.reshape(parents * 8, samples),
                imag_part.reshape(parents * 8, samples),
            ],
            axis=1,
        ).astype(BF16)
        far = dot(operator, received, ((1,), (1,)))
        out_rows = pl.ds(r, rows, stride=rhs)
        out_ref[out_rows, :] = far + near_ref[out_rows, :]


def halo(shard):
    devices = lax.axis_size(ALL)
    up = [(i, i + 1) for i in range(devices - 1)]
    down = [(j, i) for i, j in up]
    return lax.ppermute(shard, ALL, up), lax.ppermute(shard, ALL, down)


def near_field(first, base, before, currents, after, near_index, near_count, tiles, given, after_this):
    rows, boxes = currents.shape
    _, slots, basis, _, _ = tiles.shape
    rhs = rows // (2 * basis)
    start = first_slot(first)
    count = FIRST_SLOTS if first else slots - FIRST_SLOTS
    whole = lambda shape: pl.BlockSpec(shape, lambda p, base: (0,) * len(shape))
    in_specs = [whole((rows, boxes))] * 3 + [
        whole((slots, boxes)),
        whole((1, boxes)),
        pl.BlockSpec((2, 1, basis, basis, boxes), lambda p, base: (0, p + start, 0, 0, 0)),
    ]
    operands = [before, currents, after, near_index, near_count, tiles]
    if not first:
        in_specs.append(whole((rows, boxes)))
        operands.append(given)
    return pl.pallas_call(
        functools.partial(near_kernel, first),
        grid_spec=pltpu.PrefetchScalarGridSpec(
            num_scalar_prefetch=1,
            grid=(count,),
            in_specs=in_specs,
            out_specs=whole((rows, boxes)),
            scratch_shapes=[
                pltpu.VMEM((rows, 3 * boxes), BF16),
                pltpu.VMEM((3, basis * rhs, boxes), F32),
                pltpu.VMEM((2, rhs, basis, boxes), F32),
            ],
        ),
        out_shape=jax.ShapeDtypeStruct((rows, boxes), F32),
        compiler_params=params(),
        name="near_first" if first else "near_rest",
    )(base, *operands)


def body(
    currents,
    tiles,
    near_index,
    near_count,
    radiation,
    interp,
    shift_phase,
    trans_table,
    trans_kind,
    trans_target,
    inter_count,
):
    _, basis, rhs, boxes = currents.shape
    samples = radiation.shape[1]
    fine = interp.shape[0]
    parents = boxes // 8
    slots, all_parents = trans_kind.shape
    kinds = trans_table.shape[1]
    padded_kinds = -(-kinds // 128) * 128
    sources = all_parents // lax.axis_size("box")
    devices = lax.axis_size(ALL)
    rows = 2 * basis * rhs

    flat = currents.reshape(rows, boxes)
    before, after = halo(flat)
    rad = jnp.swapaxes(radiation, 1, 2)
    shifted = pl.pallas_call(
        leaf_kernel,
        in_specs=[vmem_spec()] * 3,
        out_specs=vmem_spec(),
        out_shape=jax.ShapeDtypeStruct((rhs, parents, 2 * samples), BF16),
        scratch_shapes=[pltpu.VMEM((rows, boxes), F32)],
        compiler_params=params(),
        name="leaf",
    )(flat, rad, shift_phase)
    own = lax.all_to_all(shifted, "dir", split_axis=0, concat_axis=0, tiled=True)

    table = jnp.swapaxes(trans_table, 0, 1).reshape(kinds, 2 * fine).astype(BF16)
    table = jnp.pad(table, ((0, padded_kinds - kinds), (0, 0)))
    box = lax.axis_index("box").astype(jnp.int32).reshape(1)
    whole = lambda shape: pl.BlockSpec(shape, lambda i, box: (0,) * len(shape))
    column = lambda height: pl.BlockSpec((height, sources), lambda i, box: (0, box[0]))
    part = pl.pallas_call(
        translate_kernel,
        grid_spec=pltpu.PrefetchScalarGridSpec(
            num_scalar_prefetch=1,
            grid=(1,),
            in_specs=[
                whole((sources, 2 * samples)),
                whole((fine, samples)),
                whole((padded_kinds, 2 * fine)),
                column(slots),
                column(slots),
                column(1),
            ],
            out_specs=whole((all_parents, 2 * samples)),
            scratch_shapes=[
                pltpu.VMEM((slots * sources, 2 * samples), BF16),
                pltpu.VMEM((all_parents, slots * sources), BF16),
            ],
        ),
        out_shape=jax.ShapeDtypeStruct((all_parents, 2 * samples), BF16),
        compiler_params=params(),
        name="translate",
    )(
        box,
        own.reshape(sources, 2 * samples),
        interp,
        table,
        trans_kind,
        trans_target,
        inter_count.reshape(1, all_parents),
    )
    parts = lax.all_to_all(
        part.reshape(devices, parents, 2 * samples), ALL, split_axis=0, concat_axis=0, tiled=True
    )

    base = (lax.axis_index(ALL) * boxes).astype(jnp.int32).reshape(1)
    near_args = (base, before, flat, after, near_index, near_count.reshape(1, boxes), tiles)
    near = near_field(True, *near_args, None, None)
    near = near_field(False, *near_args, near, None)

    field = pl.pallas_call(
        field_kernel,
        in_specs=[vmem_spec()] * 4,
        out_specs=vmem_spec(),
        out_shape=jax.ShapeDtypeStruct((rows, boxes), F32),
        compiler_params=params(),
        name="field",
    )(parts, rad, shift_phase, near)
    return field.reshape(2, basis, rhs, boxes)


def solution(mesh):
    return jax.shard_map(
        body,
        mesh=mesh,
        in_specs=(
            P(None, None, None, ALL),
            P(None, None, None, None, ALL),
            P(None, ALL),
            P(ALL),
            P(),
            P(),
            P(),
            P(),
            P(),
            P(),
            P(),
        ),
        out_specs=P(None, None, None, ALL),
        check_vma=False,
    )
```

```python
import jax
import jax.numpy as jnp
from jax import lax
from jax.experimental import pallas as pl
from jax.experimental.pallas import tpu as pltpu
from jax.sharding import PartitionSpec as P

F32 = jnp.float32
BF16 = jnp.bfloat16
ALL = ("box", "dir")
GROUP = 4
VMEM_LIMIT = 48 * 1024 * 1024


def vmem_spec():
    return pl.BlockSpec(memory_space=pltpu.VMEM)


def any_spec():
    return pl.BlockSpec(memory_space=pl.ANY)


def params(**more):
    return pltpu.CompilerParams(vmem_limit_bytes=VMEM_LIMIT, **more)


def dot(a, b, dims):
    return lax.dot_general(a, b, (dims, ((), ())), preferred_element_type=F32)


def leaf_kernel(cur_hbm, rad_hbm, phase_hbm, out_ref, wide_ref, cur_ref, rad_ref, phase_ref, sems):
    rhs, parents, _ = out_ref.shape
    rows = cur_ref.shape[0] // rhs
    pairs = ((cur_hbm, cur_ref), (rad_hbm, rad_ref), (phase_hbm, phase_ref))
    copies = [pltpu.make_async_copy(a, b, sems.at[i]) for i, (a, b) in enumerate(pairs)]
    for copy in copies:
        copy.start()
    for copy in copies:
        copy.wait()
    wide_ref[...] = cur_ref[...].astype(F32)
    rad_re, rad_im = rad_ref[0], rad_ref[1]
    operator = jnp.concatenate(
        [
            jnp.concatenate([rad_re, rad_im], axis=1),
            jnp.concatenate([-rad_im, rad_re], axis=1),
        ],
        axis=0,
    )
    samples = rad_re.shape[1]
    phase_re, phase_im = phase_ref[0][None], phase_ref[1][None]
    for r in range(rhs):
        vector = wide_ref[pl.ds(r, rows, stride=rhs), :].astype(BF16)
        leaf = dot(vector, operator, ((0,), (0,)))
        leaf_re = leaf[:, :samples].reshape(parents, 8, samples)
        leaf_im = leaf[:, samples:].reshape(parents, 8, samples)
        shifted_re = jnp.sum(phase_re * leaf_re - phase_im * leaf_im, axis=1)
        shifted_im = jnp.sum(phase_re * leaf_im + phase_im * leaf_re, axis=1)
        out_ref[r] = jnp.concatenate([shifted_re, shifted_im], axis=1).astype(BF16)


def translate_kernel(
    box_ref, src_ref, interp_ref, table_ref, kind_ref, target_ref, count_ref, before_ref, after_ref, out_ref, pair_ref, hot_ref
):
    del box_ref, before_ref, after_ref
    sources, double = src_ref.shape
    samples = double // 2
    slots = kind_ref.shape[0]
    targets = out_ref.shape[0]
    fine = interp_ref.shape[0]
    kinds = table_ref.shape[0]
    interp = interp_ref[...]
    parent_re = dot(src_ref[:, :samples], interp, ((1,), (1,))).astype(BF16).astype(F32)
    parent_im = dot(src_ref[:, samples:], interp, ((1,), (1,))).astype(BF16).astype(F32)
    kind_columns = jnp.transpose(kind_ref[...].astype(F32)).astype(jnp.int32)
    kind_iota = lax.broadcasted_iota(jnp.int32, (sources, kinds), 1)
    target_iota = lax.broadcasted_iota(jnp.int32, (targets, sources), 0)
    count = count_ref[...]
    for s in range(0, slots, GROUP):
        hots = [kind_iota == kind_columns[:, t : t + 1] for t in range(s, s + GROUP)]
        hot = jnp.concatenate([h.astype(F32).astype(BF16) for h in hots], axis=0)
        factor = dot(hot, table_ref[...], ((1,), (0,)))
        factor_re = factor[:, :fine].reshape(GROUP, sources, fine)
        factor_im = factor[:, fine:].reshape(GROUP, sources, fine)
        real_part = factor_re * parent_re[None] - factor_im * parent_im[None]
        imag_part = factor_re * parent_im[None] + factor_im * parent_re[None]
        real_part = real_part.astype(BF16).reshape(GROUP * sources, fine)
        imag_part = imag_part.astype(BF16).reshape(GROUP * sources, fine)
        rows = pl.ds(s * sources, GROUP * sources)
        pair_ref[rows, :samples] = dot(real_part, interp, ((1,), (0,))).astype(BF16)
        pair_ref[rows, samples:] = dot(imag_part, interp, ((1,), (0,))).astype(BF16)
    for s in range(slots):
        target = jnp.where(s < count, target_ref[s : s + 1, :], -1)
        hot_ref[:, pl.ds(s * sources, sources)] = (target_iota == target).astype(F32).astype(BF16)
    step = 512
    for t in range(0, targets, step):
        total = dot(hot_ref[pl.ds(t, step), :], pair_ref[...], ((1,), (0,)))
        out_ref[pl.ds(t, step), :] = total.astype(BF16)


def near_kernel(
    base_ref, before_ref, cur_ref, after_ref, index_ref, count_ref, tiles_ref, out_ref, buf_ref, all_ref, field_ref, sum_ref, sems
):
    boxes = cur_ref.shape[1]
    _, slots, basis, _, _ = tiles_ref.shape
    rhs = cur_ref.shape[0] // (2 * basis)
    half = basis * rhs

    def tile_copy(c, s):
        return pltpu.make_async_copy(tiles_ref.at[c, s], buf_ref.at[c, s], sems.at[c, s])

    for s in range(slots):
        for c in range(2):
            tile_copy(c, s).start()
    all_ref[:, :boxes] = before_ref[...]
    all_ref[:, boxes : 2 * boxes] = cur_ref[...]
    all_ref[:, 2 * boxes :] = after_ref[...]
    iota = lax.broadcasted_iota(jnp.int32, (3 * boxes, boxes), 0)
    for s in range(0, slots, 2):
        hots = []
        for t in (s, s + 1):
            index = index_ref[t : t + 1, :] - (base_ref[0] - boxes)
            index = jnp.where(t < count_ref[...], index, -1)
            hots.append((iota == index).astype(F32).astype(BF16))
        picked = dot(all_ref[...], jnp.concatenate(hots, axis=1), ((1,), (0,)))
        for t in range(2):
            part = picked[:, t * boxes : (t + 1) * boxes]
            vec_re, vec_im = part[:half], part[half:]
            field_ref[s + t, 0] = vec_re
            field_ref[s + t, 1] = vec_im - vec_re
            field_ref[s + t, 2] = vec_re + vec_im
    sum_ref[...] = jnp.zeros_like(sum_ref)
    high = 8

    def slot_body(s, carry):
        for c in range(2):
            tile_copy(c, s).wait()
        for m in range(0, basis, high):

            def step(n, sums):
                tile_re = buf_ref[0, s, n, pl.ds(m, high), :].astype(F32)
                tile_im = buf_ref[1, s, n, pl.ds(m, high), :].astype(F32)
                tile_sum = tile_re + tile_im
                sums = list(sums)
                for r in range(rhs):
                    row = pl.ds(n * rhs + r, 1)
                    sums[3 * r] += tile_sum * field_ref[s, 0, row, :]
                    sums[3 * r + 1] += tile_re * field_ref[s, 1, row, :]
                    sums[3 * r + 2] += tile_im * field_ref[s, 2, row, :]
                return tuple(sums)

            zero = jnp.zeros((high, boxes), F32)
            sums = lax.fori_loop(0, basis, step, (zero,) * (3 * rhs), unroll=8)
            for r in range(rhs):
                sum_ref[0, r, pl.ds(m, high), :] += sums[3 * r] - sums[3 * r + 2]
                sum_ref[1, r, pl.ds(m, high), :] += sums[3 * r] + sums[3 * r + 1]
        return carry

    lax.fori_loop(0, slots, slot_body, 0)
    for c in range(2):
        for r in range(rhs):
            out_ref[pl.ds(c * half + r, basis, stride=rhs), :] = sum_ref[c, r]


def field_kernel(part_ref, rad_ref, phase_ref, near_ref, out_ref):
    devices, parents, double = part_ref.shape
    samples = double // 2
    rhs = 8
    rad_re, rad_im = rad_ref[0], rad_ref[1]
    operator = jnp.concatenate(
        [
            jnp.concatenate([rad_re, -rad_im], axis=1),
            jnp.concatenate([rad_im, rad_re], axis=1),
        ],
        axis=0,
    )
    rows = operator.shape[0]
    phase_re, phase_im = phase_ref[0][None], phase_ref[1][None]
    for r in range(rhs):
        anter = part_ref[r].astype(F32)
        for i in range(r + rhs, devices, rhs):
            anter += part_ref[i].astype(F32)
        anter_re = anter[:, None, :samples]
        anter_im = anter[:, None, samples:]
        real_part = phase_re * anter_re + phase_im * anter_im
        imag_part = phase_re * anter_im - phase_im * anter_re
        received = jnp.concatenate(
            [
                real_part.reshape(parents * 8, samples),
                imag_part.reshape(parents * 8, samples),
            ],
            axis=1,
        ).astype(BF16)
        far = dot(operator, received, ((1,), (1,)))
        out_rows = pl.ds(r, rows, stride=rhs)
        out_ref[out_rows, :] = far + near_ref[out_rows, :]


def halo(shard):
    devices = lax.axis_size(ALL)
    up = [(i, i + 1) for i in range(devices - 1)]
    down = [(j, i) for i, j in up]
    return lax.ppermute(shard, ALL, up), lax.ppermute(shard, ALL, down)


def near_field(base, before, currents, after, near_index, near_count, tiles):
    rows, boxes = currents.shape
    _, slots, basis, _, _ = tiles.shape
    rhs = rows // (2 * basis)
    return pl.pallas_call(
        near_kernel,
        in_specs=[pl.BlockSpec(memory_space=pltpu.SMEM)] + [vmem_spec()] * 5 + [any_spec()],
        out_specs=vmem_spec(),
        out_shape=jax.ShapeDtypeStruct((rows, boxes), F32),
        scratch_shapes=[
            pltpu.VMEM((2, slots, basis, basis, boxes), BF16),
            pltpu.VMEM((rows, 3 * boxes), BF16),
            pltpu.VMEM((slots, 3, basis * rhs, boxes), F32),
            pltpu.VMEM((2, rhs, basis, boxes), F32),
            pltpu.SemaphoreType.DMA((2, slots)),
        ],
        compiler_params=params(),
        name="near",
    )(base, before, currents, after, near_index, near_count, tiles)


def body(
    currents,
    tiles,
    near_index,
    near_count,
    radiation,
    interp,
    shift_phase,
    trans_table,
    trans_kind,
    trans_target,
    inter_count,
):
    _, basis, rhs, boxes = currents.shape
    samples = radiation.shape[1]
    fine = interp.shape[0]
    parents = boxes // 8
    slots, all_parents = trans_kind.shape
    kinds = trans_table.shape[1]
    padded_kinds = -(-kinds // 128) * 128
    sources = all_parents // lax.axis_size("box")
    devices = lax.axis_size(ALL)
    rows = 2 * basis * rhs

    flat = currents.reshape(rows, boxes)
    before, after = halo(flat)
    rad = jnp.swapaxes(radiation, 1, 2)
    shifted = pl.pallas_call(
        leaf_kernel,
        in_specs=[any_spec()] * 3,
        out_specs=vmem_spec(),
        out_shape=jax.ShapeDtypeStruct((rhs, parents, 2 * samples), BF16),
        scratch_shapes=[
            pltpu.VMEM((rows, boxes), F32),
            pltpu.VMEM((rows, boxes), BF16),
            pltpu.VMEM((2, basis, samples), BF16),
            pltpu.VMEM((2, 8, samples), F32),
            pltpu.SemaphoreType.DMA((3,)),
        ],
        compiler_params=params(),
        name="leaf",
    )(flat, rad, shift_phase)
    own = lax.all_to_all(shifted, "dir", split_axis=0, concat_axis=0, tiled=True)

    table = jnp.swapaxes(trans_table, 0, 1).reshape(kinds, 2 * fine).astype(BF16)
    table = jnp.pad(table, ((0, padded_kinds - kinds), (0, 0)))
    box = lax.axis_index("box").astype(jnp.int32).reshape(1)
    whole = lambda shape: pl.BlockSpec(shape, lambda i, box: (0,) * len(shape))
    column = lambda height: pl.BlockSpec((height, sources), lambda i, box: (0, box[0]))
    part = pl.pallas_call(
        translate_kernel,
        grid_spec=pltpu.PrefetchScalarGridSpec(
            num_scalar_prefetch=1,
            grid=(1,),
            in_specs=[
                whole((sources, 2 * samples)),
                whole((fine, samples)),
                whole((padded_kinds, 2 * fine)),
                column(slots),
                column(slots),
                column(1),
                any_spec(),
                any_spec(),
            ],
            out_specs=whole((all_parents, 2 * samples)),
            scratch_shapes=[
                pltpu.VMEM((slots * sources, 2 * samples), BF16),
                pltpu.VMEM((all_parents, slots * sources), BF16),
            ],
        ),
        out_shape=jax.ShapeDtypeStruct((all_parents, 2 * samples), BF16),
        compiler_params=params(),
        name="translate",
    )(
        box,
        own.reshape(sources, 2 * samples),
        interp,
        table,
        trans_kind,
        trans_target,
        inter_count.reshape(1, all_parents),
        before,
        after,
    )
    parts = lax.all_to_all(
        part.reshape(devices, parents, 2 * samples), ALL, split_axis=0, concat_axis=0, tiled=True
    )

    base = (lax.axis_index(ALL) * boxes).astype(jnp.int32).reshape(1)
    near = near_field(base, before, flat, after, near_index, near_count.reshape(1, boxes), tiles)

    field = pl.pallas_call(
        field_kernel,
        in_specs=[vmem_spec()] * 4,
        out_specs=vmem_spec(),
        out_shape=jax.ShapeDtypeStruct((rows, boxes), F32),
        compiler_params=params(),
        name="field",
    )(parts, rad, shift_phase, near)
    return field.reshape(2, basis, rhs, boxes)


def solution(mesh):
    return jax.shard_map(
        body,
        mesh=mesh,
        in_specs=(
            P(None, None, None, ALL),
            P(None, None, None, None, ALL),
            P(None, ALL),
            P(ALL),
            P(),
            P(),
            P(),
            P(),
            P(),
            P(),
            P(),
        ),
        out_specs=P(None, None, None, ALL),
        check_vma=False,
    )
```

```python
import jax
import jax.numpy as jnp
from jax import lax
from jax.experimental import pallas as pl
from jax.experimental.pallas import tpu as pltpu
from jax.sharding import PartitionSpec as P

F32 = jnp.float32
BF16 = jnp.bfloat16
ALL = ("box", "dir")
GROUP = 4
VMEM_LIMIT = 48 * 1024 * 1024
LEAF_LIMIT = 63 * 1024 * 1024


def vmem_spec():
    return pl.BlockSpec(memory_space=pltpu.VMEM)


def any_spec():
    return pl.BlockSpec(memory_space=pl.ANY)


def params(limit=VMEM_LIMIT):
    return pltpu.CompilerParams(vmem_limit_bytes=limit)


def dot(a, b, dims):
    return lax.dot_general(a, b, (dims, ((), ())), preferred_element_type=F32)


def leaf_kernel(cur_hbm, rad_hbm, phase_hbm, out_ref, wide_ref, cur_ref, rad_ref, phase_ref, sems):
    rhs, parents, _ = out_ref.shape
    rows = cur_ref.shape[0] // rhs
    pairs = ((cur_hbm, cur_ref), (rad_hbm, rad_ref), (phase_hbm, phase_ref))
    copies = [pltpu.make_async_copy(a, b, sems.at[i]) for i, (a, b) in enumerate(pairs)]
    for copy in copies:
        copy.start()
    for copy in copies:
        copy.wait()
    wide_ref[...] = cur_ref[...].astype(F32)
    rad_re, rad_im = rad_ref[0], rad_ref[1]
    operator = jnp.concatenate(
        [
            jnp.concatenate([rad_re, rad_im], axis=1),
            jnp.concatenate([-rad_im, rad_re], axis=1),
        ],
        axis=0,
    )
    samples = rad_re.shape[1]
    phase_re, phase_im = phase_ref[0][None], phase_ref[1][None]
    for r in range(rhs):
        vector = wide_ref[pl.ds(r, rows, stride=rhs), :].astype(BF16)
        leaf = dot(vector, operator, ((0,), (0,)))
        leaf_re = leaf[:, :samples].reshape(parents, 8, samples)
        leaf_im = leaf[:, samples:].reshape(parents, 8, samples)
        shifted_re = jnp.sum(phase_re * leaf_re - phase_im * leaf_im, axis=1)
        shifted_im = jnp.sum(phase_re * leaf_im + phase_im * leaf_re, axis=1)
        out_ref[r] = jnp.concatenate([shifted_re, shifted_im], axis=1).astype(BF16)


def translate_kernel(
    box_ref, src_ref, interp_ref, table_ref, kind_ref, target_ref, count_ref, inner_ref, outer_ref, out_ref, pair_ref, hot_ref
):
    del box_ref, inner_ref, outer_ref
    sources, double = src_ref.shape
    samples = double // 2
    slots = kind_ref.shape[0]
    targets = out_ref.shape[0]
    fine = interp_ref.shape[0]
    kinds = table_ref.shape[0]
    interp = interp_ref[...]
    parent_re = dot(src_ref[:, :samples], interp, ((1,), (1,))).astype(BF16).astype(F32)
    parent_im = dot(src_ref[:, samples:], interp, ((1,), (1,))).astype(BF16).astype(F32)
    kind_columns = jnp.transpose(kind_ref[...].astype(F32)).astype(jnp.int32)
    kind_iota = lax.broadcasted_iota(jnp.int32, (sources, kinds), 1)
    target_iota = lax.broadcasted_iota(jnp.int32, (targets, sources), 0)
    count = count_ref[...]
    for s in range(0, slots, GROUP):
        hots = [kind_iota == kind_columns[:, t : t + 1] for t in range(s, s + GROUP)]
        hot = jnp.concatenate([h.astype(F32).astype(BF16) for h in hots], axis=0)
        factor = dot(hot, table_ref[...], ((1,), (0,)))
        factor_re = factor[:, :fine].reshape(GROUP, sources, fine)
        factor_im = factor[:, fine:].reshape(GROUP, sources, fine)
        real_part = factor_re * parent_re[None] - factor_im * parent_im[None]
        imag_part = factor_re * parent_im[None] + factor_im * parent_re[None]
        real_part = real_part.astype(BF16).reshape(GROUP * sources, fine)
        imag_part = imag_part.astype(BF16).reshape(GROUP * sources, fine)
        rows = pl.ds(s * sources, GROUP * sources)
        pair_ref[rows, :samples] = dot(real_part, interp, ((1,), (0,))).astype(BF16)
        pair_ref[rows, samples:] = dot(imag_part, interp, ((1,), (0,))).astype(BF16)
    for s in range(slots):
        target = jnp.where(s < count, target_ref[s : s + 1, :], -1)
        hot_ref[:, pl.ds(s * sources, sources)] = (target_iota == target).astype(F32).astype(BF16)
    step = 512
    for t in range(0, targets, step):
        total = dot(hot_ref[pl.ds(t, step), :], pair_ref[...], ((1,), (0,)))
        out_ref[pl.ds(t, step), :] = total.astype(BF16)


def near_kernel(
    base_ref, inner_ref, cur_ref, outer_ref, index_ref, count_ref, tiles_ref, out_ref, buf_ref, all_ref, field_ref, sum_ref, sems
):
    boxes = cur_ref.shape[1]
    _, slots, basis, _, _ = tiles_ref.shape
    rhs = cur_ref.shape[0] // (2 * basis)
    half = basis * rhs

    def tile_copy(c, s):
        return pltpu.make_async_copy(tiles_ref.at[c, s], buf_ref.at[c, s], sems.at[c, s])

    for s in range(slots):
        for c in range(2):
            tile_copy(c, s).start()
    all_ref[:, :boxes] = inner_ref[...]
    all_ref[:, boxes : 2 * boxes] = cur_ref[...]
    all_ref[:, 2 * boxes :] = outer_ref[...]
    base = base_ref[0]
    even = jnp.where((base // boxes) % 2 == 0, 1, 0)
    iota = lax.broadcasted_iota(jnp.int32, (3 * boxes, boxes), 0)
    for s in range(0, slots, 2):
        hots = []
        for t in (s, s + 1):
            index = index_ref[t : t + 1, :] - (base - boxes)
            swapped = jnp.where(index < boxes, index + 2 * boxes, index - 2 * boxes)
            own = jnp.logical_and(index >= boxes, index < 2 * boxes)
            index = jnp.where(jnp.logical_or(own, even == 0), index, swapped)
            index = jnp.where(t < count_ref[...], index, -1)
            hots.append((iota == index).astype(F32).astype(BF16))
        picked = dot(all_ref[...], jnp.concatenate(hots, axis=1), ((1,), (0,)))
        for t in range(2):
            part = picked[:, t * boxes : (t + 1) * boxes]
            vec_re, vec_im = part[:half], part[half:]
            field_ref[s + t, 0] = vec_re
            field_ref[s + t, 1] = vec_im - vec_re
            field_ref[s + t, 2] = vec_re + vec_im
    sum_ref[...] = jnp.zeros_like(sum_ref)
    high = 8

    def slot_body(s, carry):
        for c in range(2):
            tile_copy(c, s).wait()
        for m in range(0, basis, high):

            def step(n, sums):
                tile_re = buf_ref[0, s, n, pl.ds(m, high), :].astype(F32)
                tile_im = buf_ref[1, s, n, pl.ds(m, high), :].astype(F32)
                tile_sum = tile_re + tile_im
                sums = list(sums)
                for r in range(rhs):
                    row = pl.ds(n * rhs + r, 1)
                    sums[3 * r] += tile_sum * field_ref[s, 0, row, :]
                    sums[3 * r + 1] += tile_re * field_ref[s, 1, row, :]
                    sums[3 * r + 2] += tile_im * field_ref[s, 2, row, :]
                return tuple(sums)

            zero = jnp.zeros((high, boxes), F32)
            sums = lax.fori_loop(0, basis, step, (zero,) * (3 * rhs), unroll=8)
            for r in range(rhs):
                sum_ref[0, r, pl.ds(m, high), :] += sums[3 * r] - sums[3 * r + 2]
                sum_ref[1, r, pl.ds(m, high), :] += sums[3 * r] + sums[3 * r + 1]
        return carry

    lax.fori_loop(0, slots, slot_body, 0)
    for c in range(2):
        for r in range(rhs):
            out_ref[pl.ds(c * half + r, basis, stride=rhs), :] = sum_ref[c, r]


def field_kernel(part_ref, rad_ref, phase_ref, near_ref, out_ref):
    devices, parents, double = part_ref.shape
    samples = double // 2
    rhs = 8
    rad_re, rad_im = rad_ref[0], rad_ref[1]
    operator = jnp.concatenate(
        [
            jnp.concatenate([rad_re, -rad_im], axis=1),
            jnp.concatenate([rad_im, rad_re], axis=1),
        ],
        axis=0,
    )
    rows = operator.shape[0]
    phase_re, phase_im = phase_ref[0][None], phase_ref[1][None]
    for r in range(rhs):
        anter = part_ref[r].astype(F32)
        for i in range(r + rhs, devices, rhs):
            anter += part_ref[i].astype(F32)
        anter_re = anter[:, None, :samples]
        anter_im = anter[:, None, samples:]
        real_part = phase_re * anter_re + phase_im * anter_im
        imag_part = phase_re * anter_im - phase_im * anter_re
        received = jnp.concatenate(
            [
                real_part.reshape(parents * 8, samples),
                imag_part.reshape(parents * 8, samples),
            ],
            axis=1,
        ).astype(BF16)
        far = dot(operator, received, ((1,), (1,)))
        out_rows = pl.ds(r, rows, stride=rhs)
        out_ref[out_rows, :] = far + near_ref[out_rows, :]


def halo(shard):
    devices = lax.axis_size(ALL)
    swaps = []
    for first in (0, 1):
        up = [(i, i + 1) for i in range(first, devices - 1, 2)]
        swaps.append(lax.ppermute(shard, ALL, up + [(j, i) for i, j in up]))
    return swaps


def near_field(base, inner, currents, outer, near_index, near_count, tiles):
    rows, boxes = currents.shape
    _, slots, basis, _, _ = tiles.shape
    rhs = rows // (2 * basis)
    return pl.pallas_call(
        near_kernel,
        in_specs=[pl.BlockSpec(memory_space=pltpu.SMEM)] + [vmem_spec()] * 5 + [any_spec()],
        out_specs=vmem_spec(),
        out_shape=jax.ShapeDtypeStruct((rows, boxes), F32),
        scratch_shapes=[
            pltpu.VMEM((2, slots, basis, basis, boxes), BF16),
            pltpu.VMEM((rows, 3 * boxes), BF16),
            pltpu.VMEM((slots, 3, basis * rhs, boxes), F32),
            pltpu.VMEM((2, rhs, basis, boxes), F32),
            pltpu.SemaphoreType.DMA((2, slots)),
        ],
        compiler_params=params(),
        name="near",
    )(base, inner, currents, outer, near_index, near_count, tiles)


def body(
    currents,
    tiles,
    near_index,
    near_count,
    radiation,
    interp,
    shift_phase,
    trans_table,
    trans_kind,
    trans_target,
    inter_count,
):
    _, basis, rhs, boxes = currents.shape
    samples = radiation.shape[1]
    fine = interp.shape[0]
    parents = boxes // 8
    slots, all_parents = trans_kind.shape
    kinds = trans_table.shape[1]
    padded_kinds = -(-kinds // 128) * 128
    sources = all_parents // lax.axis_size("box")
    devices = lax.axis_size(ALL)
    rows = 2 * basis * rhs

    flat = currents.reshape(rows, boxes)
    inner, outer = halo(flat)
    rad = jnp.swapaxes(radiation, 1, 2)
    shifted = pl.pallas_call(
        leaf_kernel,
        in_specs=[any_spec()] * 3,
        out_specs=vmem_spec(),
        out_shape=jax.ShapeDtypeStruct((rhs, parents, 2 * samples), BF16),
        scratch_shapes=[
            pltpu.VMEM((rows, boxes), F32),
            pltpu.VMEM((rows, boxes), BF16),
            pltpu.VMEM((2, basis, samples), BF16),
            pltpu.VMEM((2, 8, samples), F32),
            pltpu.SemaphoreType.DMA((3,)),
        ],
        compiler_params=params(LEAF_LIMIT),
        name="leaf",
    )(flat, rad, shift_phase)
    own = lax.all_to_all(shifted, "dir", split_axis=0, concat_axis=0, tiled=True)

    table = jnp.swapaxes(trans_table, 0, 1).reshape(kinds, 2 * fine).astype(BF16)
    table = jnp.pad(table, ((0, padded_kinds - kinds), (0, 0)))
    box = lax.axis_index("box").astype(jnp.int32).reshape(1)
    whole = lambda shape: pl.BlockSpec(shape, lambda i, box: (0,) * len(shape))
    column = lambda height: pl.BlockSpec((height, sources), lambda i, box: (0, box[0]))
    part = pl.pallas_call(
        translate_kernel,
        grid_spec=pltpu.PrefetchScalarGridSpec(
            num_scalar_prefetch=1,
            grid=(1,),
            in_specs=[
                whole((sources, 2 * samples)),
                whole((fine, samples)),
                whole((padded_kinds, 2 * fine)),
                column(slots),
                column(slots),
                column(1),
                any_spec(),
                any_spec(),
            ],
            out_specs=whole((all_parents, 2 * samples)),
            scratch_shapes=[
                pltpu.VMEM((slots * sources, 2 * samples), BF16),
                pltpu.VMEM((all_parents, slots * sources), BF16),
            ],
        ),
        out_shape=jax.ShapeDtypeStruct((all_parents, 2 * samples), BF16),
        compiler_params=params(),
        name="translate",
    )(
        box,
        own.reshape(sources, 2 * samples),
        interp,
        table,
        trans_kind,
        trans_target,
        inter_count.reshape(1, all_parents),
        inner,
        outer,
    )
    parts = lax.all_to_all(
        part.reshape(devices, parents, 2 * samples), ALL, split_axis=0, concat_axis=0, tiled=True
    )

    base = (lax.axis_index(ALL) * boxes).astype(jnp.int32).reshape(1)
    near = near_field(base, inner, flat, outer, near_index, near_count.reshape(1, boxes), tiles)

    field = pl.pallas_call(
        field_kernel,
        in_specs=[vmem_spec()] * 4,
        out_specs=vmem_spec(),
        out_shape=jax.ShapeDtypeStruct((rows, boxes), F32),
        compiler_params=params(),
        name="field",
    )(parts, rad, shift_phase, near)
    return field.reshape(2, basis, rhs, boxes)


def solution(mesh):
    return jax.shard_map(
        body,
        mesh=mesh,
        in_specs=(
            P(None, None, None, ALL),
            P(None, None, None, None, ALL),
            P(None, ALL),
            P(ALL),
            P(),
            P(),
            P(),
            P(),
            P(),
            P(),
            P(),
        ),
        out_specs=P(None, None, None, ALL),
        check_vma=False,
    )
```

```python
import jax
import jax.numpy as jnp
from jax import lax
from jax.experimental import pallas as pl
from jax.experimental.pallas import tpu as pltpu
from jax.sharding import PartitionSpec as P

F32 = jnp.float32
BF16 = jnp.bfloat16
ALL = ("box", "dir")
GROUP = 4
VMEM_LIMIT = 48 * 1024 * 1024
LEAF_LIMIT = 63 * 1024 * 1024


def vmem_spec():
    return pl.BlockSpec(memory_space=pltpu.VMEM)


def any_spec():
    return pl.BlockSpec(memory_space=pl.ANY)


def params(limit=VMEM_LIMIT):
    return pltpu.CompilerParams(vmem_limit_bytes=limit)


def dot(a, b, dims):
    return lax.dot_general(a, b, (dims, ((), ())), preferred_element_type=F32)


def leaf_kernel(cur_hbm, rad_hbm, phase_hbm, out_ref, wide_ref, cur_ref, rad_ref, phase_ref, sems):
    rhs, parents, _ = out_ref.shape
    rows = cur_ref.shape[0] // rhs
    pairs = ((cur_hbm, cur_ref), (rad_hbm, rad_ref), (phase_hbm, phase_ref))
    copies = [pltpu.make_async_copy(a, b, sems.at[i]) for i, (a, b) in enumerate(pairs)]
    for copy in copies:
        copy.start()
    for copy in copies:
        copy.wait()
    wide_ref[...] = cur_ref[...].astype(F32)
    rad_re, rad_im = rad_ref[0], rad_ref[1]
    operator = jnp.concatenate(
        [
            jnp.concatenate([rad_re, rad_im], axis=1),
            jnp.concatenate([-rad_im, rad_re], axis=1),
        ],
        axis=0,
    )
    samples = rad_re.shape[1]
    phase_re, phase_im = phase_ref[0][None], phase_ref[1][None]
    for r in range(rhs):
        vector = wide_ref[pl.ds(r, rows, stride=rhs), :].astype(BF16)
        leaf = dot(vector, operator, ((0,), (0,)))
        leaf_re = leaf[:, :samples].reshape(parents, 8, samples)
        leaf_im = leaf[:, samples:].reshape(parents, 8, samples)
        shifted_re = jnp.sum(phase_re * leaf_re - phase_im * leaf_im, axis=1)
        shifted_im = jnp.sum(phase_re * leaf_im + phase_im * leaf_re, axis=1)
        out_ref[r] = jnp.concatenate([shifted_re, shifted_im], axis=1).astype(BF16)


def translate_kernel(
    box_ref, src_ref, interp_ref, table_ref, kind_ref, target_ref, count_ref, inner_ref, outer_ref, out_ref, pair_ref, hot_ref, pick_ref, product_ref
):
    del box_ref, inner_ref, outer_ref
    sources, double = src_ref.shape
    samples = double // 2
    slots = kind_ref.shape[0]
    targets = out_ref.shape[0]
    fine = interp_ref.shape[0]
    kinds = table_ref.shape[0]
    interp = interp_ref[...]
    parent_re = dot(src_ref[:, :samples], interp, ((1,), (1,))).astype(BF16).astype(F32)
    parent_im = dot(src_ref[:, samples:], interp, ((1,), (1,))).astype(BF16).astype(F32)
    kind_columns = jnp.transpose(kind_ref[...].astype(F32)).astype(jnp.int32)
    kind_iota = lax.broadcasted_iota(jnp.int32, (sources, kinds), 1)
    target_iota = lax.broadcasted_iota(jnp.int32, (targets, sources), 0)
    count = count_ref[...]
    for s in range(slots):
        hot = (kind_iota == kind_columns[:, s : s + 1]).astype(F32).astype(BF16)
        pick_ref[pl.ds(s * sources, sources), :] = hot
    height = GROUP * sources
    half = fine // 2
    for s in range(0, slots, GROUP):
        rows = pl.ds(s * sources, height)
        for k in range(0, fine, half):
            hot = pick_ref[rows, :]
            low, high = slice(k, k + half), slice(fine + k, fine + k + half)
            factor_re = dot(hot, table_ref[:, low], ((1,), (0,))).reshape(GROUP, sources, half)
            factor_im = dot(hot, table_ref[:, high], ((1,), (0,))).reshape(GROUP, sources, half)
            vec_re, vec_im = parent_re[None, :, low], parent_im[None, :, low]
            real_part = (factor_re * vec_re - factor_im * vec_im).astype(BF16)
            imag_part = (factor_re * vec_im + factor_im * vec_re).astype(BF16)
            product_ref[rows, low] = real_part.reshape(height, half)
            product_ref[rows, high] = imag_part.reshape(height, half)
        pair_ref[rows, :samples] = dot(product_ref[rows, :fine], interp, ((1,), (0,))).astype(BF16)
        pair_ref[rows, samples:] = dot(product_ref[rows, fine:], interp, ((1,), (0,))).astype(BF16)
    for s in range(slots):
        target = jnp.where(s < count, target_ref[s : s + 1, :], -1)
        hot_ref[:, pl.ds(s * sources, sources)] = (target_iota == target).astype(F32).astype(BF16)
    step = 512
    for t in range(0, targets, step):
        total = dot(hot_ref[pl.ds(t, step), :], pair_ref[...], ((1,), (0,)))
        out_ref[pl.ds(t, step), :] = total.astype(BF16)


def near_kernel(
    base_ref, inner_ref, cur_ref, outer_ref, index_ref, count_ref, tiles_ref, out_ref, buf_ref, all_ref, field_ref, sum_ref, sems
):
    boxes = cur_ref.shape[1]
    _, slots, basis, _, _ = tiles_ref.shape
    rhs = cur_ref.shape[0] // (2 * basis)
    half = basis * rhs

    def tile_copy(c, s):
        return pltpu.make_async_copy(tiles_ref.at[c, s], buf_ref.at[c, s], sems.at[c, s])

    for s in range(slots):
        for c in range(2):
            tile_copy(c, s).start()
    all_ref[:, :boxes] = inner_ref[...]
    all_ref[:, boxes : 2 * boxes] = cur_ref[...]
    all_ref[:, 2 * boxes :] = outer_ref[...]
    base = base_ref[0]
    even = jnp.where((base // boxes) % 2 == 0, 1, 0)
    iota = lax.broadcasted_iota(jnp.int32, (3 * boxes, boxes), 0)
    for s in range(0, slots, 2):
        hots = []
        for t in (s, s + 1):
            index = index_ref[t : t + 1, :] - (base - boxes)
            swapped = jnp.where(index < boxes, index + 2 * boxes, index - 2 * boxes)
            own = jnp.logical_and(index >= boxes, index < 2 * boxes)
            index = jnp.where(jnp.logical_or(own, even == 0), index, swapped)
            index = jnp.where(t < count_ref[...], index, -1)
            hots.append((iota == index).astype(F32).astype(BF16))
        picked = dot(all_ref[...], jnp.concatenate(hots, axis=1), ((1,), (0,)))
        for t in range(2):
            part = picked[:, t * boxes : (t + 1) * boxes]
            vec_re, vec_im = part[:half], part[half:]
            field_ref[s + t, 0] = vec_re
            field_ref[s + t, 1] = vec_im - vec_re
            field_ref[s + t, 2] = vec_re + vec_im
    sum_ref[...] = jnp.zeros_like(sum_ref)
    high = 8

    def slot_body(s, carry):
        for c in range(2):
            tile_copy(c, s).wait()
        for m in range(0, basis, high):

            def step(n, sums):
                tile_re = buf_ref[0, s, n, pl.ds(m, high), :].astype(F32)
                tile_im = buf_ref[1, s, n, pl.ds(m, high), :].astype(F32)
                tile_sum = tile_re + tile_im
                sums = list(sums)
                for r in range(rhs):
                    row = pl.ds(n * rhs + r, 1)
                    sums[3 * r] += tile_sum * field_ref[s, 0, row, :]
                    sums[3 * r + 1] += tile_re * field_ref[s, 1, row, :]
                    sums[3 * r + 2] += tile_im * field_ref[s, 2, row, :]
                return tuple(sums)

            zero = jnp.zeros((high, boxes), F32)
            sums = lax.fori_loop(0, basis, step, (zero,) * (3 * rhs), unroll=16)
            for r in range(rhs):
                sum_ref[0, r, pl.ds(m, high), :] += sums[3 * r] - sums[3 * r + 2]
                sum_ref[1, r, pl.ds(m, high), :] += sums[3 * r] + sums[3 * r + 1]
        return carry

    lax.fori_loop(0, slots, slot_body, 0)
    for c in range(2):
        for r in range(rhs):
            out_ref[pl.ds(c * half + r, basis, stride=rhs), :] = sum_ref[c, r]


def field_kernel(part_ref, rad_ref, phase_ref, near_ref, out_ref):
    devices, parents, double = part_ref.shape
    samples = double // 2
    rhs = 8
    rad_re, rad_im = rad_ref[0], rad_ref[1]
    operator = jnp.concatenate(
        [
            jnp.concatenate([rad_re, -rad_im], axis=1),
            jnp.concatenate([rad_im, rad_re], axis=1),
        ],
        axis=0,
    )
    rows = operator.shape[0]
    phase_re, phase_im = phase_ref[0][None], phase_ref[1][None]
    for r in range(rhs):
        anter = part_ref[r].astype(F32)
        for i in range(r + rhs, devices, rhs):
            anter += part_ref[i].astype(F32)
        anter_re = anter[:, None, :samples]
        anter_im = anter[:, None, samples:]
        real_part = phase_re * anter_re + phase_im * anter_im
        imag_part = phase_re * anter_im - phase_im * anter_re
        received = jnp.concatenate(
            [
                real_part.reshape(parents * 8, samples),
                imag_part.reshape(parents * 8, samples),
            ],
            axis=1,
        ).astype(BF16)
        far = dot(operator, received, ((1,), (1,)))
        out_rows = pl.ds(r, rows, stride=rhs)
        out_ref[out_rows, :] = far + near_ref[out_rows, :]


def halo(shard):
    devices = lax.axis_size(ALL)
    inner = [(i, i + 1 if i % 2 == 0 else i - 1) for i in range(devices)]
    outer = [(i, (i + 1 if i % 2 else i - 1) % devices) for i in range(devices)]
    outer_block = lax.ppermute(shard, ALL, outer)
    shard, outer_block = lax.optimization_barrier((shard, outer_block))
    return lax.ppermute(shard, ALL, inner), outer_block


def near_field(base, inner, currents, outer, near_index, near_count, tiles):
    rows, boxes = currents.shape
    _, slots, basis, _, _ = tiles.shape
    rhs = rows // (2 * basis)
    return pl.pallas_call(
        near_kernel,
        in_specs=[pl.BlockSpec(memory_space=pltpu.SMEM)] + [vmem_spec()] * 5 + [any_spec()],
        out_specs=vmem_spec(),
        out_shape=jax.ShapeDtypeStruct((rows, boxes), F32),
        scratch_shapes=[
            pltpu.VMEM((2, slots, basis, basis, boxes), BF16),
            pltpu.VMEM((rows, 3 * boxes), BF16),
            pltpu.VMEM((slots, 3, basis * rhs, boxes), F32),
            pltpu.VMEM((2, rhs, basis, boxes), F32),
            pltpu.SemaphoreType.DMA((2, slots)),
        ],
        compiler_params=params(),
        name="near",
    )(base, inner, currents, outer, near_index, near_count, tiles)


def body(
    currents,
    tiles,
    near_index,
    near_count,
    radiation,
    interp,
    shift_phase,
    trans_table,
    trans_kind,
    trans_target,
    inter_count,
):
    _, basis, rhs, boxes = currents.shape
    samples = radiation.shape[1]
    fine = interp.shape[0]
    parents = boxes // 8
    slots, all_parents = trans_kind.shape
    kinds = trans_table.shape[1]
    padded_kinds = -(-kinds // 128) * 128
    sources = all_parents // lax.axis_size("box")
    devices = lax.axis_size(ALL)
    rows = 2 * basis * rhs

    flat = currents.reshape(rows, boxes)
    inner, outer = halo(flat)
    rad = jnp.swapaxes(radiation, 1, 2)
    shifted = pl.pallas_call(
        leaf_kernel,
        in_specs=[any_spec()] * 3,
        out_specs=vmem_spec(),
        out_shape=jax.ShapeDtypeStruct((rhs, parents, 2 * samples), BF16),
        scratch_shapes=[
            pltpu.VMEM((rows, boxes), F32),
            pltpu.VMEM((rows, boxes), BF16),
            pltpu.VMEM((2, basis, samples), BF16),
            pltpu.VMEM((2, 8, samples), F32),
            pltpu.SemaphoreType.DMA((3,)),
        ],
        compiler_params=params(LEAF_LIMIT),
        name="leaf",
    )(flat, rad, shift_phase)
    own = lax.all_to_all(shifted, "dir", split_axis=0, concat_axis=0, tiled=True)

    table = jnp.swapaxes(trans_table, 0, 1).reshape(kinds, 2 * fine).astype(BF16)
    table = jnp.pad(table, ((0, padded_kinds - kinds), (0, 0)))
    box = lax.axis_index("box").astype(jnp.int32).reshape(1)
    whole = lambda shape: pl.BlockSpec(shape, lambda i, box: (0,) * len(shape))
    column = lambda height: pl.BlockSpec((height, sources), lambda i, box: (0, box[0]))
    part = pl.pallas_call(
        translate_kernel,
        grid_spec=pltpu.PrefetchScalarGridSpec(
            num_scalar_prefetch=1,
            grid=(1,),
            in_specs=[
                whole((sources, 2 * samples)),
                whole((fine, samples)),
                whole((padded_kinds, 2 * fine)),
                column(slots),
                column(slots),
                column(1),
                any_spec(),
                any_spec(),
            ],
            out_specs=whole((all_parents, 2 * samples)),
            scratch_shapes=[
                pltpu.VMEM((slots * sources, 2 * samples), BF16),
                pltpu.VMEM((all_parents, slots * sources), BF16),
                pltpu.VMEM((slots * sources, padded_kinds), BF16),
                pltpu.VMEM((slots * sources, 2 * fine), BF16),
            ],
        ),
        out_shape=jax.ShapeDtypeStruct((all_parents, 2 * samples), BF16),
        compiler_params=params(),
        name="translate",
    )(
        box,
        own.reshape(sources, 2 * samples),
        interp,
        table,
        trans_kind,
        trans_target,
        inter_count.reshape(1, all_parents),
        inner,
        outer,
    )
    parts = lax.all_to_all(
        part.reshape(devices, parents, 2 * samples), ALL, split_axis=0, concat_axis=0, tiled=True
    )

    base = (lax.axis_index(ALL) * boxes).astype(jnp.int32).reshape(1)
    near = near_field(base, inner, flat, outer, near_index, near_count.reshape(1, boxes), tiles)

    field = pl.pallas_call(
        field_kernel,
        in_specs=[vmem_spec()] * 4,
        out_specs=vmem_spec(),
        out_shape=jax.ShapeDtypeStruct((rows, boxes), F32),
        compiler_params=params(),
        name="field",
    )(parts, rad, shift_phase, near)
    return field.reshape(2, basis, rhs, boxes)


def solution(mesh):
    return jax.shard_map(
        body,
        mesh=mesh,
        in_specs=(
            P(None, None, None, ALL),
            P(None, None, None, None, ALL),
            P(None, ALL),
            P(ALL),
            P(),
            P(),
            P(),
            P(),
            P(),
            P(),
            P(),
        ),
        out_specs=P(None, None, None, ALL),
        check_vma=False,
    )
```

```python
import jax
import jax.numpy as jnp
from jax import lax
from jax.experimental import pallas as pl
from jax.experimental.pallas import tpu as pltpu
from jax.sharding import PartitionSpec as P

F32 = jnp.float32
BF16 = jnp.bfloat16
ALL = ("box", "dir")
GROUP = 4
EARLY = 4
VMEM_LIMIT = 48 * 1024 * 1024
LOOKUP_LIMIT = 20 * 1024 * 1024
LEAF_LIMIT = 63 * 1024 * 1024


def vmem_spec():
    return pl.BlockSpec(memory_space=pltpu.VMEM)


def any_spec():
    return pl.BlockSpec(memory_space=pl.ANY)


def params(limit=VMEM_LIMIT):
    return pltpu.CompilerParams(vmem_limit_bytes=limit)


def dot(a, b, dims):
    return lax.dot_general(a, b, (dims, ((), ())), preferred_element_type=F32)


def leaf_kernel(cur_hbm, rad_hbm, phase_hbm, out_ref, wide_ref, cur_ref, rad_ref, phase_ref, sems):
    rhs, parents, _ = out_ref.shape
    rows = cur_ref.shape[0] // rhs
    pairs = ((cur_hbm, cur_ref), (rad_hbm, rad_ref), (phase_hbm, phase_ref))
    copies = [pltpu.make_async_copy(a, b, sems.at[i]) for i, (a, b) in enumerate(pairs)]
    for copy in copies:
        copy.start()
    for copy in copies:
        copy.wait()
    wide_ref[...] = cur_ref[...].astype(F32)
    rad_re, rad_im = rad_ref[0], rad_ref[1]
    operator = jnp.concatenate(
        [
            jnp.concatenate([rad_re, rad_im], axis=1),
            jnp.concatenate([-rad_im, rad_re], axis=1),
        ],
        axis=0,
    )
    samples = rad_re.shape[1]
    phase_re, phase_im = phase_ref[0][None], phase_ref[1][None]
    for r in range(rhs):
        vector = wide_ref[pl.ds(r, rows, stride=rhs), :].astype(BF16)
        leaf = dot(vector, operator, ((0,), (0,)))
        leaf_re = leaf[:, :samples].reshape(parents, 8, samples)
        leaf_im = leaf[:, samples:].reshape(parents, 8, samples)
        shifted_re = jnp.sum(phase_re * leaf_re - phase_im * leaf_im, axis=1)
        shifted_im = jnp.sum(phase_re * leaf_im + phase_im * leaf_re, axis=1)
        out_ref[r] = jnp.concatenate([shifted_re, shifted_im], axis=1).astype(BF16)


def lookup_kernel(box_ref, table_ref, kind_ref, out_ref, pick_ref):
    pairs, kinds = pick_ref.shape
    slots = EARLY
    sources = pairs // slots
    columns = pl.ds(pl.multiple_of(box_ref[0] * sources, sources), sources)
    kind_columns = jnp.transpose(kind_ref[:, columns].astype(F32)).astype(jnp.int32)
    kind_iota = lax.broadcasted_iota(jnp.int32, (sources, kinds), 1)
    for s in range(slots):
        hot = (kind_iota == kind_columns[:, s : s + 1]).astype(F32).astype(BF16)
        pick_ref[pl.ds(s * sources, sources), :] = hot
    height = GROUP * sources
    for s in range(0, pairs, height):
        out_ref[pl.ds(s, height), :] = dot(pick_ref[pl.ds(s, height), :], table_ref[...], ((1,), (0,))).astype(BF16)


def translate_kernel(
    box_ref, src_ref, interp_ref, table_ref, kind_ref, factor_ref, target_ref, count_ref, inner_ref, outer_ref, out_ref, pair_ref, hot_ref, pick_ref, product_ref
):
    del box_ref, inner_ref, outer_ref
    sources, double = src_ref.shape
    samples = double // 2
    slots = kind_ref.shape[0]
    targets = out_ref.shape[0]
    fine = interp_ref.shape[0]
    kinds = table_ref.shape[0]
    interp = interp_ref[...]
    parent_re = dot(src_ref[:, :samples], interp, ((1,), (1,))).astype(BF16).astype(F32)
    parent_im = dot(src_ref[:, samples:], interp, ((1,), (1,))).astype(BF16).astype(F32)
    kind_columns = jnp.transpose(kind_ref[...].astype(F32)).astype(jnp.int32)
    kind_iota = lax.broadcasted_iota(jnp.int32, (sources, kinds), 1)
    target_iota = lax.broadcasted_iota(jnp.int32, (targets, sources), 0)
    count = count_ref[...]
    for s in range(slots):
        hot = (kind_iota == kind_columns[:, s : s + 1]).astype(F32).astype(BF16)
        pick_ref[pl.ds(s * sources, sources), :] = hot
    height = GROUP * sources
    half = fine // 2
    for s in range(0, slots, GROUP):
        rows = pl.ds(s * sources, height)
        for k in range(0, fine, half):
            low, high = slice(k, k + half), slice(fine + k, fine + k + half)
            if s < EARLY:
                factor_re, factor_im = factor_ref[rows, low].astype(F32), factor_ref[rows, high].astype(F32)
            else:
                hot = pick_ref[rows, :]
                factor_re = dot(hot, table_ref[:, low], ((1,), (0,)))
                factor_im = dot(hot, table_ref[:, high], ((1,), (0,)))
            factor_re = factor_re.reshape(GROUP, sources, half)
            factor_im = factor_im.reshape(GROUP, sources, half)
            vec_re, vec_im = parent_re[None, :, low], parent_im[None, :, low]
            real_part = (factor_re * vec_re - factor_im * vec_im).astype(BF16)
            imag_part = (factor_re * vec_im + factor_im * vec_re).astype(BF16)
            product_ref[rows, low] = real_part.reshape(height, half)
            product_ref[rows, high] = imag_part.reshape(height, half)
        pair_ref[rows, :samples] = dot(product_ref[rows, :fine], interp, ((1,), (0,))).astype(BF16)
        pair_ref[rows, samples:] = dot(product_ref[rows, fine:], interp, ((1,), (0,))).astype(BF16)
    for s in range(slots):
        target = jnp.where(s < count, target_ref[s : s + 1, :], -1)
        hot_ref[:, pl.ds(s * sources, sources)] = (target_iota == target).astype(F32).astype(BF16)
    step = 512
    for t in range(0, targets, step):
        total = dot(hot_ref[pl.ds(t, step), :], pair_ref[...], ((1,), (0,)))
        out_ref[pl.ds(t, step), :] = total.astype(BF16)


def near_kernel(
    base_ref, inner_ref, cur_ref, outer_ref, index_ref, count_ref, tiles_ref, out_ref, buf_ref, all_ref, field_ref, sum_ref, sems
):
    boxes = cur_ref.shape[1]
    _, slots, basis, _, _ = tiles_ref.shape
    rhs = cur_ref.shape[0] // (2 * basis)
    half = basis * rhs

    def tile_copy(c, s):
        return pltpu.make_async_copy(tiles_ref.at[c, s], buf_ref.at[c, s], sems.at[c, s])

    for s in range(slots):
        for c in range(2):
            tile_copy(c, s).start()
    all_ref[:, :boxes] = inner_ref[...]
    all_ref[:, boxes : 2 * boxes] = cur_ref[...]
    all_ref[:, 2 * boxes :] = outer_ref[...]
    base = base_ref[0]
    even = jnp.where((base // boxes) % 2 == 0, 1, 0)
    iota = lax.broadcasted_iota(jnp.int32, (3 * boxes, boxes), 0)
    for s in range(0, slots, 2):
        hots = []
        for t in (s, s + 1):
            index = index_ref[t : t + 1, :] - (base - boxes)
            swapped = jnp.where(index < boxes, index + 2 * boxes, index - 2 * boxes)
            own = jnp.logical_and(index >= boxes, index < 2 * boxes)
            index = jnp.where(jnp.logical_or(own, even == 0), index, swapped)
            index = jnp.where(t < count_ref[...], index, -1)
            hots.append((iota == index).astype(F32).astype(BF16))
        picked = dot(all_ref[...], jnp.concatenate(hots, axis=1), ((1,), (0,)))
        for t in range(2):
            part = picked[:, t * boxes : (t + 1) * boxes]
            vec_re, vec_im = part[:half], part[half:]
            field_ref[s + t, 0] = vec_re
            field_ref[s + t, 1] = vec_im - vec_re
            field_ref[s + t, 2] = vec_re + vec_im
    sum_ref[...] = jnp.zeros_like(sum_ref)
    high = 8

    def slot_body(s, carry):
        for c in range(2):
            tile_copy(c, s).wait()
        for m in range(0, basis, high):

            def step(n, sums):
                tile_re = buf_ref[0, s, n, pl.ds(m, high), :].astype(F32)
                tile_im = buf_ref[1, s, n, pl.ds(m, high), :].astype(F32)
                tile_sum = tile_re + tile_im
                sums = list(sums)
                for r in range(rhs):
                    row = pl.ds(n * rhs + r, 1)
                    sums[3 * r] += tile_sum * field_ref[s, 0, row, :]
                    sums[3 * r + 1] += tile_re * field_ref[s, 1, row, :]
                    sums[3 * r + 2] += tile_im * field_ref[s, 2, row, :]
                return tuple(sums)

            zero = jnp.zeros((high, boxes), F32)
            sums = lax.fori_loop(0, basis, step, (zero,) * (3 * rhs), unroll=16)
            for r in range(rhs):
                sum_ref[0, r, pl.ds(m, high), :] += sums[3 * r] - sums[3 * r + 2]
                sum_ref[1, r, pl.ds(m, high), :] += sums[3 * r] + sums[3 * r + 1]
        return carry

    lax.fori_loop(0, slots, slot_body, 0)
    for c in range(2):
        for r in range(rhs):
            out_ref[pl.ds(c * half + r, basis, stride=rhs), :] = sum_ref[c, r]


def field_kernel(part_ref, rad_ref, phase_ref, near_ref, out_ref):
    devices, parents, double = part_ref.shape
    samples = double // 2
    rhs = 8
    rad_re, rad_im = rad_ref[0], rad_ref[1]
    operator = jnp.concatenate(
        [
            jnp.concatenate([rad_re, -rad_im], axis=1),
            jnp.concatenate([rad_im, rad_re], axis=1),
        ],
        axis=0,
    )
    rows = operator.shape[0]
    phase_re, phase_im = phase_ref[0][None], phase_ref[1][None]
    for r in range(rhs):
        anter = part_ref[r].astype(F32)
        for i in range(r + rhs, devices, rhs):
            anter += part_ref[i].astype(F32)
        anter_re = anter[:, None, :samples]
        anter_im = anter[:, None, samples:]
        real_part = phase_re * anter_re + phase_im * anter_im
        imag_part = phase_re * anter_im - phase_im * anter_re
        received = jnp.concatenate(
            [
                real_part.reshape(parents * 8, samples),
                imag_part.reshape(parents * 8, samples),
            ],
            axis=1,
        ).astype(BF16)
        far = dot(operator, received, ((1,), (1,)))
        out_rows = pl.ds(r, rows, stride=rhs)
        out_ref[out_rows, :] = far + near_ref[out_rows, :]


def halo(shard):
    devices = lax.axis_size(ALL)
    inner = [(i, i + 1 if i % 2 == 0 else i - 1) for i in range(devices)]
    outer = [(i, (i + 1 if i % 2 else i - 1) % devices) for i in range(devices)]
    outer_block = lax.ppermute(shard, ALL, outer)
    shard, outer_block = lax.optimization_barrier((shard, outer_block))
    return lax.ppermute(shard, ALL, inner), outer_block


def near_field(base, inner, currents, outer, near_index, near_count, tiles):
    rows, boxes = currents.shape
    _, slots, basis, _, _ = tiles.shape
    rhs = rows // (2 * basis)
    return pl.pallas_call(
        near_kernel,
        in_specs=[pl.BlockSpec(memory_space=pltpu.SMEM)] + [vmem_spec()] * 5 + [any_spec()],
        out_specs=vmem_spec(),
        out_shape=jax.ShapeDtypeStruct((rows, boxes), F32),
        scratch_shapes=[
            pltpu.VMEM((2, slots, basis, basis, boxes), BF16),
            pltpu.VMEM((rows, 3 * boxes), BF16),
            pltpu.VMEM((slots, 3, basis * rhs, boxes), F32),
            pltpu.VMEM((2, rhs, basis, boxes), F32),
            pltpu.SemaphoreType.DMA((2, slots)),
        ],
        compiler_params=params(),
        name="near",
    )(base, inner, currents, outer, near_index, near_count, tiles)


def body(
    currents,
    tiles,
    near_index,
    near_count,
    radiation,
    interp,
    shift_phase,
    trans_table,
    trans_kind,
    trans_target,
    inter_count,
):
    _, basis, rhs, boxes = currents.shape
    samples = radiation.shape[1]
    fine = interp.shape[0]
    parents = boxes // 8
    slots, all_parents = trans_kind.shape
    kinds = trans_table.shape[1]
    padded_kinds = -(-kinds // 128) * 128
    sources = all_parents // lax.axis_size("box")
    devices = lax.axis_size(ALL)
    rows = 2 * basis * rhs

    flat = currents.reshape(rows, boxes)
    inner, outer = halo(flat)
    rad = jnp.swapaxes(radiation, 1, 2)
    shifted = pl.pallas_call(
        leaf_kernel,
        in_specs=[any_spec()] * 3,
        out_specs=vmem_spec(),
        out_shape=jax.ShapeDtypeStruct((rhs, parents, 2 * samples), BF16),
        scratch_shapes=[
            pltpu.VMEM((rows, boxes), F32),
            pltpu.VMEM((rows, boxes), BF16),
            pltpu.VMEM((2, basis, samples), BF16),
            pltpu.VMEM((2, 8, samples), F32),
            pltpu.SemaphoreType.DMA((3,)),
        ],
        compiler_params=params(LEAF_LIMIT),
        name="leaf",
    )(flat, rad, shift_phase)
    own = lax.all_to_all(shifted, "dir", split_axis=0, concat_axis=0, tiled=True)

    table = jnp.swapaxes(trans_table, 0, 1).reshape(kinds, 2 * fine).astype(BF16)
    table = jnp.pad(table, ((0, padded_kinds - kinds), (0, 0)))
    box = lax.axis_index("box").astype(jnp.int32).reshape(1)
    whole = lambda shape: pl.BlockSpec(shape, lambda i, box: (0,) * len(shape))
    column = lambda height: pl.BlockSpec((height, sources), lambda i, box: (0, box[0]))
    factor = pl.pallas_call(
        lookup_kernel,
        in_specs=[pl.BlockSpec(memory_space=pltpu.SMEM)] + [vmem_spec()] * 2,
        out_specs=vmem_spec(),
        out_shape=jax.ShapeDtypeStruct((EARLY * sources, 2 * fine), BF16),
        scratch_shapes=[pltpu.VMEM((EARLY * sources, padded_kinds), BF16)],
        compiler_params=params(LOOKUP_LIMIT),
        name="lookup",
    )(box, table, trans_kind)
    part = pl.pallas_call(
        translate_kernel,
        grid_spec=pltpu.PrefetchScalarGridSpec(
            num_scalar_prefetch=1,
            grid=(1,),
            in_specs=[
                whole((sources, 2 * samples)),
                whole((fine, samples)),
                whole((padded_kinds, 2 * fine)),
                column(slots),
                vmem_spec(),
                column(slots),
                column(1),
                any_spec(),
                any_spec(),
            ],
            out_specs=whole((all_parents, 2 * samples)),
            scratch_shapes=[
                pltpu.VMEM((slots * sources, 2 * samples), BF16),
                pltpu.VMEM((all_parents, slots * sources), BF16),
                pltpu.VMEM((slots * sources, padded_kinds), BF16),
                pltpu.VMEM((slots * sources, 2 * fine), BF16),
            ],
        ),
        out_shape=jax.ShapeDtypeStruct((all_parents, 2 * samples), BF16),
        compiler_params=params(),
        name="translate",
    )(
        box,
        own.reshape(sources, 2 * samples),
        interp,
        table,
        trans_kind,
        factor,
        trans_target,
        inter_count.reshape(1, all_parents),
        inner,
        outer,
    )
    parts = lax.all_to_all(
        part.reshape(devices, parents, 2 * samples), ALL, split_axis=0, concat_axis=0, tiled=True
    )

    base = (lax.axis_index(ALL) * boxes).astype(jnp.int32).reshape(1)
    near = near_field(base, inner, flat, outer, near_index, near_count.reshape(1, boxes), tiles)

    field = pl.pallas_call(
        field_kernel,
        in_specs=[vmem_spec()] * 4,
        out_specs=vmem_spec(),
        out_shape=jax.ShapeDtypeStruct((rows, boxes), F32),
        compiler_params=params(),
        name="field",
    )(parts, rad, shift_phase, near)
    return field.reshape(2, basis, rhs, boxes)


def solution(mesh):
    return jax.shard_map(
        body,
        mesh=mesh,
        in_specs=(
            P(None, None, None, ALL),
            P(None, None, None, None, ALL),
            P(None, ALL),
            P(ALL),
            P(),
            P(),
            P(),
            P(),
            P(),
            P(),
            P(),
        ),
        out_specs=P(None, None, None, ALL),
        check_vma=False,
    )
```
